32 devices in a mesh: ctx: 2 (over core), head: 4 (over y, x), exp: 4 (over z).
Axes of the slice: x: 2, y: 2, z: 4, core: 2. Of those that a mesh axis runs over, the one named last changes fastest.
Arguments:
- query_heads: bfloat16 [4, 4, 256, 4, 512], P('exp', None, 'ctx', 'head'), may hold values from -180 to 180
- key_heads: bfloat16 [4, 4, 256, 4, 128], P('exp', None, 'ctx', 'head'), may hold values from -6 to 6
- value_heads: bfloat16 [4, 4, 256, 4, 128], P('exp', None, 'ctx', 'head'), may hold values from -6 to 6
- hidden_state: bfloat16 [4, 4, 256, 2048], P('exp', 'head', 'ctx'), may hold values from -6 to 6
- output_grad: bfloat16 [4, 4, 256, 2048], P('exp', 'head', 'ctx'), may hold values from -6 to 6
- norm_gain: float32 [2048], replicated, may hold values from 0.5 to 1.5
- expert_ids: int32 [4, 4, 256, 8], P('exp', 'head', 'ctx'), may hold values from 0 to 31, all different within a row; in each aligned block of 128 rows (0 to 127, 128 to 255, ..., all dimensions but the last counted through in order) at most 36 rows name the same one
- gate_probs: float32 [4, 4, 256, 8], P('exp', 'head', 'ctx'), may hold values from 0.02 to 0.4
- out_weight: bfloat16 [4, 512, 2048], P('head'), may hold values from -0.125 to 0.125
- gate_weight: bfloat16 [32, 2048, 768], P(('ctx', 'head', 'exp')), may hold values from -0.125 to 0.125
- up_weight: bfloat16 [32, 2048, 768], P(('ctx', 'head', 'exp')), may hold values from -0.125 to 0.125
- down_weight: bfloat16 [32, 768, 2048], P(('ctx', 'head', 'exp')), may hold values from -0.21875 to 0.21875
Outputs:
- query_gradient: bfloat16 [4, 4, 256, 4, 512], P('exp', None, 'ctx', 'head')
- key_gradient: bfloat16 [4, 4, 256, 4, 128], P('exp', None, 'ctx', 'head')
- value_gradient: bfloat16 [4, 4, 256, 4, 128], P('exp', None, 'ctx', 'head')
- hidden_grad: bfloat16 [4, 4, 256, 2048], P('exp', 'head', 'ctx')
- gain_grad: float32 [2048], replicated
- proj_grad: bfloat16 [4, 512, 2048], P('head', ('ctx', 'exp'))
- gate_grad: bfloat16 [32, 2048, 768], P(('ctx', 'head', 'exp'))
- up_grad: bfloat16 [32, 2048, 768], P(('ctx', 'head', 'exp'))
- down_grad: bfloat16 [32, 768, 2048], P(('ctx', 'head', 'exp'))
The draws below stay inside these ranges and needn't reach their ends.
Inputs may be any that keep to these rules, and one draw needn't show every extreme that they name: `expert_ids`: each token names 8 different experts; the 128 tokens of one sequence on one index of ctx name one expert at most 36 times, and some such group names some expert exactly 36 times.
All inputs are finite; a program needn't handle non-finite values.
Results may differ from the reference program's by a relative error of at most 0.034.
Values may be sent and summed in bfloat16 or wider, within the bound.
A program may use at most 192 MiB of HBM per device.

```python
import math
import jax
import jax.numpy as jnp
import numpy as np
from jax import lax

D = 2048
FF = 768
HD = 128
KV_HEADS = 4
Q_PER_KV = 4
TOP = 8
TOK_DEV = 128
SEQS = 4
SEQ_LEN = 256
EXPERTS = 32
CAP = 36
N_EXP = 4
DEVICES = 32


def paired_draw(key):
    key_shape = (N_EXP, SEQS, SEQ_LEN, KV_HEADS, HD)
    query_shape = (N_EXP, SEQS, SEQ_LEN, KV_HEADS, Q_PER_KV * HD)
    base_keys = jnp.clip(jax.random.normal(jax.random.fold_in(key, 11), key_shape, jnp.float32), -6.0, 6.0)
    base_queries = jnp.clip(jax.random.normal(jax.random.fold_in(key, 12), query_shape, jnp.float32), -6.0, 6.0)
    key_vals = base_keys
    query_vals = base_queries
    return (query_vals, key_vals)


def draw_query_heads(key, part):
    query_vals, key_vals = paired_draw(key)
    return query_vals.astype(jnp.bfloat16)


def draw_key_heads(key, part):
    query_vals, key_vals = paired_draw(key)
    return key_vals.astype(jnp.bfloat16)


def block_levels(key, shape, split, smallest, high):
    loudness = 1.0
    for position, shards_of in split:
        heights = jax.random.uniform(jax.random.fold_in(jax.random.fold_in(key, 6), position), (shards_of,), jnp.float32, smallest / len(split), high / len(split))
        loudness = loudness * jnp.repeat(jnp.exp(heights), shape[position] // shards_of).reshape((-1,) + (1,) * (len(shape) - 1 - position))
    return loudness


def shared_out(stream_key, own, number, rows, count, top, reach, slope):
    order = jax.random.permutation(stream_key, count)
    crowded, ordinary = load_shares(count, rows * top, reach, slope, True), load_shares(count, rows * top, reach, slope, False)
    places = jnp.arange(count)

    def named(lengths, offset_by):
        used = int((lengths > 0).sum())
        fixed = max(1, used // 4)
        passed = fixed + (places - fixed + offset_by * (used - fixed)) % max(1, count - fixed)
        return jnp.zeros((count,), jnp.int32).at[order[jnp.where(places < fixed, places, passed)]].set(jnp.asarray(lengths, jnp.int32))

    lengths = jnp.where(number % 4 == 0, named(crowded, number // 4), named(ordinary, number - number // 4 - 1))
    mixed = jax.random.permutation(jax.random.fold_in(own, 3), count)
    donor, taker = mixed[0:count // 2 * 2:2], mixed[1:count // 2 * 2:2]
    room = jnp.minimum(lengths[donor] - 1, reach - lengths[taker]) // 2
    room = jnp.where((donor == order[0]) | (taker == order[0]) | (lengths[taker] == 0), 0, jnp.maximum(room, 0))
    passed = jax.random.randint(jax.random.fold_in(own, 4), (count // 2,), 0, 1 << 20) % (room + 1)
    lengths = lengths.at[donor].add(-passed).at[taker].add(passed)
    members = jnp.searchsorted(jnp.cumsum(lengths), jnp.arange(rows * top), side="right").astype(jnp.int32)
    grid = members.reshape(top, rows).T
    grid = grid[jax.random.permutation(jax.random.fold_in(own, 1), rows)]
    offset_by = jax.random.randint(jax.random.fold_in(own, 2), (rows, 1), 0, top)
    return jnp.take_along_axis(grid, (jnp.arange(top)[None, :] + offset_by) % top, axis=1)


def load_shares(number_of, total, most, skew, full):
    portions = [(1 << 20) // math.isqrt(grade ** skew) + 1 for grade in range(1, number_of + 1)]
    largest = most if full else min(most, max(-(-total // number_of), total * portions[0] // sum(portions)))
    least = 1 if total - largest >= number_of - 1 else 0
    given, surplus = [largest] + [least] * (number_of - 1), total - largest - least * (number_of - 1)
    while surplus > 0:
        movable = [i for i in range(1, number_of) if given[i] < largest] or [i for i in range(1, number_of) if given[i] < most]
        whole, budget = sum([portions[i] for i in movable]), surplus
        for i in movable:
            more = min(most - given[i], max(1, budget * portions[i] // whole), surplus)
            given[i] = given[i] + more
            surplus = surplus - more
    return np.array(given)


def normal_values(key, shape, deviation, bound, cuts=(), kind=jnp.bfloat16):
    factor_of = block_levels(key, shape, cuts, -0.22, 0.18) if cuts else 1.0
    result = jax.random.normal(key, shape, jnp.float32) * deviation * factor_of
    return jnp.minimum(jnp.maximum(result, -bound), bound).astype(kind)


def setup_inputs(seed: int = 0) -> dict:
    streams_of = jax.random.split(jax.random.key(seed), 13)
    query_heads = draw_query_heads(jax.random.fold_in(streams_of[12], 71), 0)
    key_heads = draw_key_heads(jax.random.fold_in(streams_of[12], 71), 0)
    value_heads = normal_values(streams_of[2], (N_EXP, SEQS, SEQ_LEN, KV_HEADS, HD), 1.0, 6.0, ((0, 4), (2, 2), (3, 4)))
    hidden_state = normal_values(streams_of[3], (N_EXP, SEQS, SEQ_LEN, D), 1.0, 6.0, ((0, 4), (1, 4), (2, 2)))
    output_grad = normal_values(streams_of[4], (N_EXP, SEQS, SEQ_LEN, D), 1.0, 6.0, ((0, 4), (1, 4), (2, 2)))
    norm_gain = jnp.clip(1.0 + 0.1 * jax.random.normal(streams_of[5], (D,), jnp.float32), 0.5, 1.5)
    expert_ids_keys = jax.random.split(jax.random.fold_in(streams_of[6], 1), N_EXP * SEQS * SEQ_LEN // TOK_DEV)
    expert_ids_turns = jax.random.permutation(jax.random.fold_in(streams_of[6], 3), N_EXP * SEQS * SEQ_LEN // TOK_DEV)
    expert_ids = jax.vmap(lambda own, number: shared_out(jax.random.fold_in(streams_of[6], 2), own, number, TOK_DEV, EXPERTS, TOP, CAP, 2))(expert_ids_keys, expert_ids_turns).reshape((N_EXP, SEQS, SEQ_LEN, TOP))
    gate_probs = jnp.clip(jnp.exp(math.log(0.4) - 2.9957323 * jax.random.uniform(streams_of[7], (N_EXP, SEQS, SEQ_LEN, TOP), jnp.float32) ** block_levels(streams_of[7], (N_EXP, SEQS, SEQ_LEN, TOP), ((0, 4), (1, 4), (2, 2)), -0.2, 0.2)), 0.02, 0.4)
    out_weight = normal_values(streams_of[8], (KV_HEADS, Q_PER_KV * HD, D), (KV_HEADS * Q_PER_KV * HD) ** -0.5, 0.125, ((0, 4),))
    gate_weight = normal_values(streams_of[9], (EXPERTS, D, FF), D ** -0.5, 0.125, ((0, 32),))
    up_weight = normal_values(streams_of[10], (EXPERTS, D, FF), D ** -0.5, 0.125, ((0, 32),))
    down_weight = normal_values(streams_of[11], (EXPERTS, FF, D), FF ** -0.5, 0.21875, ((0, 32),))
    return dict(query_heads=query_heads, key_heads=key_heads, value_heads=value_heads, hidden_state=hidden_state, output_grad=output_grad, norm_gain=norm_gain, expert_ids=expert_ids, gate_probs=gate_probs, out_weight=out_weight, gate_weight=gate_weight, up_weight=up_weight, down_weight=down_weight)


NORM_EPS = 1e-06
ROWS_DIMS = (((0,), (0,)), ((), ()))
LAST_DIMS = (((1,), (1,)), ((), ()))

def rounded_result(values):
    return lax.optimization_barrier(values.astype(jnp.bfloat16)).astype(jnp.float32)

def expert_backward(inputs, upstream, gate_mat, up_mat, down_mat):
    gate_val = jnp.dot(inputs, gate_mat, preferred_element_type=jnp.float32)
    up_val = jnp.dot(inputs, up_mat, preferred_element_type=jnp.float32)
    grad_act = lax.dot_general(upstream, down_mat, LAST_DIMS, preferred_element_type=jnp.float32)
    sigma_gate = jax.nn.sigmoid(gate_val)
    act_rows = (gate_val * sigma_gate * up_val).astype(jnp.bfloat16)
    up_part = (grad_act * gate_val * sigma_gate).astype(jnp.bfloat16)
    gate_part = (grad_act * up_val * sigma_gate * (1.0 + gate_val * (1.0 - sigma_gate))).astype(jnp.bfloat16)
    down_sum = lax.dot_general(act_rows, upstream, ROWS_DIMS, preferred_element_type=jnp.float32)
    gate_sum = lax.dot_general(inputs, gate_part, ROWS_DIMS, preferred_element_type=jnp.float32)
    up_sum = lax.dot_general(inputs, up_part, ROWS_DIMS, preferred_element_type=jnp.float32)
    back_rows = lax.dot_general(gate_part, gate_mat, LAST_DIMS, preferred_element_type=jnp.float32) + lax.dot_general(up_part, up_mat, LAST_DIMS, preferred_element_type=jnp.float32)
    return (back_rows.astype(jnp.bfloat16), gate_sum, up_sum, down_sum)

def reference(query_heads, key_heads, value_heads, hidden_state, output_grad, norm_gain, expert_ids, gate_probs, out_weight, gate_weight, up_weight, down_weight):
    token_count = N_EXP * SEQS * SEQ_LEN
    hidden_wide = hidden_state.reshape(token_count, D).astype(jnp.float32)
    out_rows = output_grad.reshape(token_count, D)
    inv_rms = lax.rsqrt(lax.optimization_barrier(jnp.mean(hidden_wide * hidden_wide, axis=1, keepdims=True)) + NORM_EPS)
    unit_rows = hidden_wide * inv_rms
    gain_wide = norm_gain.astype(jnp.float32)
    normed = (unit_rows * gain_wide).astype(jnp.bfloat16)
    flat_ids = expert_ids.reshape(-1).astype(jnp.int32)
    flat_probs = gate_probs.reshape(-1).astype(jnp.float32)
    row_limit = DEVICES * CAP
    ranked = jnp.argsort(flat_ids, stable=True).astype(jnp.int32)
    ranked = jnp.concatenate([ranked, jnp.zeros((row_limit,), jnp.int32)])
    counts = jnp.bincount(flat_ids, length=EXPERTS).astype(jnp.int32)
    starts = (jnp.cumsum(counts) - counts).astype(jnp.int32)

    def one_expert(grad_sum, pieces):
        gate_mat, up_mat, down_mat, first_row, amount = pieces
        picked = lax.dynamic_slice(ranked, (first_row,), (row_limit,))
        valid_rows = (jnp.arange(row_limit, dtype=jnp.int32) < amount)[:, None]
        token_idx = (picked // TOP).astype(jnp.int32)
        inputs = jnp.where(valid_rows, normed[token_idx], jnp.zeros((), jnp.bfloat16))
        weighted = (flat_probs[picked][:, None] * out_rows[token_idx].astype(jnp.float32)).astype(jnp.bfloat16)
        upstream = jnp.where(valid_rows, weighted, jnp.zeros((), jnp.bfloat16))
        back_rows, gate_sum, up_sum, down_sum = expert_backward(inputs, upstream, gate_mat, up_mat, down_mat)
        grad_sum = grad_sum.at[token_idx].add(jnp.where(valid_rows, back_rows.astype(jnp.float32), jnp.zeros((), jnp.float32)))
        return (grad_sum, (gate_sum.astype(jnp.bfloat16), up_sum.astype(jnp.bfloat16), down_sum.astype(jnp.bfloat16)))
    normed_grad, (gate_grad, up_grad, down_grad) = lax.scan(one_expert, jnp.zeros((token_count, D), jnp.float32), (gate_weight, up_weight, down_weight, starts, counts))
    gain_grad = lax.optimization_barrier(jnp.sum(normed_grad * unit_rows, axis=0))
    scaled = normed_grad * gain_wide
    mixed_term = lax.optimization_barrier(jnp.mean(scaled * unit_rows, axis=1, keepdims=True))
    hidden_rows = (out_rows.astype(jnp.float32) + inv_rms * (scaled - unit_rows * mixed_term)).astype(jnp.bfloat16)
    seq_total = N_EXP * SEQS
    queries = query_heads.reshape(seq_total, SEQ_LEN, KV_HEADS, Q_PER_KV, HD)
    key_vals = key_heads.reshape(seq_total, SEQ_LEN, KV_HEADS, HD)
    value_vals = value_heads.reshape(seq_total, SEQ_LEN, KV_HEADS, HD)
    grad_seqs = hidden_rows.reshape(seq_total, SEQ_LEN, D)
    proj_mat = out_weight.astype(jnp.float32)
    score_scaling = HD ** (-0.5)
    causal = jnp.arange(SEQ_LEN)[:, None] >= jnp.arange(SEQ_LEN)[None, :]

    def one_sequence(proj_sum, pieces):
        query_seq, key_seq, value_seq, grad_seq = pieces
        query_broadcast = query_seq.astype(jnp.float32)
        key_broadcast = key_seq.astype(jnp.float32)
        value_broadcast = value_seq.astype(jnp.float32)
        attention_scores = jnp.einsum('qlct,ult->lcqu', query_broadcast, key_broadcast) * score_scaling
        masked = jnp.where(causal, attention_scores, -jnp.inf)
        row_peak = lax.optimization_barrier(jnp.max(masked, axis=3, keepdims=True))
        weight_matrices = jnp.exp(masked - row_peak)
        norm_total_sum = lax.optimization_barrier(jnp.sum(weight_matrices, axis=3, keepdims=True))
        attention_values = rounded_result(jnp.einsum('tbzc,cte->ztbe', weight_matrices / norm_total_sum, value_broadcast, precision=lax.Precision.HIGHEST))
        log_sum = row_peak + jnp.log(norm_total_sum)
        grad_wide = grad_seq.astype(jnp.float32)
        attention_gradient = rounded_result(jnp.einsum('pc,hec->phe', grad_wide, proj_mat)).reshape(SEQ_LEN, KV_HEADS, Q_PER_KV, HD)
        proj_sum = proj_sum + jnp.einsum('phe,pc->hec', attention_values.reshape(SEQ_LEN, KV_HEADS, Q_PER_KV * HD), grad_wide)
        delta_rows = lax.optimization_barrier(jnp.sum(attention_gradient * attention_values, axis=3))
        probability_values = jnp.where(causal, jnp.exp(attention_scores - log_sum), 0.0)
        value_gradient = jnp.einsum('nzag,anzk->gnk', rounded_result(probability_values), attention_gradient)
        probability_gradient = jnp.einsum('qlct,ult->lcqu', attention_gradient, value_broadcast)
        score_gradient = rounded_result(probability_values * (probability_gradient - delta_rows.transpose(1, 2, 0)[..., None]))
        query_gradient = jnp.einsum('tbzc,cte->ztbe', score_gradient, key_broadcast) * score_scaling
        key_gradient = jnp.einsum('nzag,anzk->gnk', score_gradient, query_broadcast) * score_scaling
        return (proj_sum, (query_gradient.astype(jnp.bfloat16), key_gradient.astype(jnp.bfloat16), value_gradient.astype(jnp.bfloat16)))
    proj_total, (query_gradient, key_gradient, value_gradient) = lax.scan(one_sequence, jnp.zeros((KV_HEADS, Q_PER_KV * HD, D), jnp.float32), (queries, key_vals, value_vals, grad_seqs))
    return (query_gradient.reshape(N_EXP, SEQS, SEQ_LEN, KV_HEADS, Q_PER_KV * HD), key_gradient.reshape(N_EXP, SEQS, SEQ_LEN, KV_HEADS, HD), value_gradient.reshape(N_EXP, SEQS, SEQ_LEN, KV_HEADS, HD), hidden_rows.reshape(N_EXP, SEQS, SEQ_LEN, D), gain_grad, proj_total.astype(jnp.bfloat16), gate_grad, up_grad, down_grad)
```

```python
import jax
import jax.numpy as jnp
from jax import lax
from jax.sharding import PartitionSpec as P

NORM_EPS = 1e-06
FLOOR_SCORE = -1e30
ROWS_DIMS = (((0,), (0,)), ((), ()))
LAST_DIMS = (((1,), (1,)), ((), ()))
HIDDEN_PIECES = 2
GRAD_PIECES = 1
BACK_PIECES = 2


def slot_capacity(token_rows, choices, experts):
    mean_load = (token_rows * choices + experts - 1) // experts
    return max(2, mean_load + max(1, mean_load // 8))


def heads_to_rows(block_vals, per_key, head_size):
    seq_count, block_len = (block_vals.shape[0], block_vals.shape[1])
    split_vals = block_vals.reshape(seq_count, block_len, per_key, head_size)
    return split_vals.transpose(0, 2, 1, 3).reshape(seq_count, per_key * block_len, head_size)


def rows_to_heads(row_vals, per_key, block_len):
    seq_count, head_size = (row_vals.shape[0], row_vals.shape[2])
    split_vals = row_vals.reshape(seq_count, per_key, block_len, head_size)
    return split_vals.transpose(0, 2, 1, 3).reshape(seq_count, block_len, per_key * head_size)


def column_pieces(rows, pieces):
    width = rows.shape[-1] // pieces
    return [rows[..., i * width : (i + 1) * width] for i in range(pieces)]


def direct_scatter(blocks, axis):
    count = lax.axis_size(axis)
    me = lax.axis_index(axis)
    total = lax.dynamic_index_in_dim(blocks, me, 0, keepdims=False)
    for step in range(1, count):
        share = lax.dynamic_index_in_dim(blocks, (me + step) % count, 0, keepdims=False)
        arrived = lax.ppermute(
            share.astype(jnp.bfloat16), axis, [(i, (i + step) % count) for i in range(count)]
        )
        total = total + arrived.astype(jnp.float32)
    return total


def direct_gather(block, axis):
    count = lax.axis_size(axis)
    me = lax.axis_index(axis)
    held = [block] + [
        lax.ppermute(block, axis, [(i, (i + step) % count) for i in range(count)])
        for step in range(1, count)
    ]
    stacked = jnp.stack(held)
    return [
        lax.dynamic_index_in_dim(stacked, (me - i) % count, 0, keepdims=False)
        for i in range(count)
    ]


def on_device(
    query_heads,
    key_heads,
    value_heads,
    hidden_state,
    output_grad,
    norm_gain,
    expert_ids,
    gate_probs,
    out_weight,
    gate_weight,
    up_weight,
    down_weight,
):
    model_width = hidden_state.shape[-1]
    token_rows = hidden_state.shape[2]
    choices = expert_ids.shape[-1]
    device_count = lax.axis_size(("ctx", "head", "exp"))
    exp_count = lax.axis_size("exp")
    plane_count = device_count // exp_count
    capacity = slot_capacity(token_rows, choices, device_count) * exp_count
    group_rows = exp_count * token_rows
    own_hidden = hidden_state.reshape(token_rows, model_width)
    out_rows = output_grad.reshape(token_rows, model_width)
    hidden_wide = own_hidden.astype(jnp.float32)
    inv_rms = lax.rsqrt(jnp.mean(hidden_wide * hidden_wide, axis=1, keepdims=True) + NORM_EPS)
    unit_rows = hidden_wide * inv_rms
    routing = jnp.concatenate(
        [
            expert_ids.reshape(token_rows, choices).astype(jnp.float32),
            gate_probs.reshape(token_rows, choices),
            inv_rms,
        ],
        axis=1,
    )
    group_routing = lax.all_gather(routing, "exp", axis=0, tiled=True)
    group_hidden = [
        lax.all_gather(piece, "exp", axis=0, tiled=True)
        for piece in column_pieces(own_hidden, HIDDEN_PIECES)
    ]
    group_grad = [
        lax.all_gather(piece, "exp", axis=0, tiled=True)
        for piece in column_pieces(out_rows, GRAD_PIECES)
    ]
    group_rms = group_routing[:, 2 * choices :]

    plane_experts = jnp.arange(plane_count, dtype=jnp.int32) * exp_count + lax.axis_index("exp")
    group_ids = group_routing[:, :choices].astype(jnp.int32)
    names = (group_ids[None, :, :] == plane_experts[:, None, None]).astype(jnp.float32)
    named = jnp.sum(names, axis=2)
    named_prob = jnp.sum(names * group_routing[None, :, choices : 2 * choices], axis=2)
    earlier = (jnp.arange(group_rows)[:, None] < jnp.arange(group_rows)[None, :]).astype(
        jnp.bfloat16
    )
    before = jnp.dot(named.astype(jnp.bfloat16), earlier, preferred_element_type=jnp.float32)
    slot_of = jnp.where(named > 0.0, before, -1.0)
    picks = slot_of[:, None, :] == jnp.arange(capacity, dtype=jnp.float32)[None, :, None]
    slot_prob = jnp.sum(jnp.where(picks, named_prob[:, None, :], 0.0), axis=2).reshape(-1, 1)
    picker = picks.astype(jnp.bfloat16).reshape(plane_count * capacity, group_rows)

    def exchange(rows):
        return lax.all_to_all(rows, ("ctx", "head"), split_axis=0, concat_axis=0, tiled=True)

    def pick(rows):
        return jnp.dot(picker, rows, preferred_element_type=jnp.float32)

    inputs = []
    for piece, gain in zip(group_hidden, column_pieces(norm_gain, HIDDEN_PIECES)):
        normed = (piece.astype(jnp.float32) * group_rms * gain).astype(jnp.bfloat16)
        inputs.append(exchange(pick(normed).astype(jnp.bfloat16)))
    upstream = [exchange((pick(piece) * slot_prob).astype(jnp.bfloat16)) for piece in group_grad]

    gate_mat, up_mat, down_mat = (gate_weight[0], up_weight[0], down_weight[0])
    x_width = model_width // HIDDEN_PIECES
    gate_val = up_val = grad_act = 0.0
    for i, piece in enumerate(inputs):
        rows = slice(i * x_width, (i + 1) * x_width)
        gate_val += jnp.dot(piece, gate_mat[rows], preferred_element_type=jnp.float32)
        up_val += jnp.dot(piece, up_mat[rows], preferred_element_type=jnp.float32)
    for piece, mat in zip(upstream, column_pieces(down_mat, GRAD_PIECES)):
        grad_act += lax.dot_general(piece, mat, LAST_DIMS, preferred_element_type=jnp.float32)
    sigma_gate = jax.nn.sigmoid(gate_val)
    act_rows = (gate_val * sigma_gate * up_val).astype(jnp.bfloat16)
    up_part = (grad_act * gate_val * sigma_gate).astype(jnp.bfloat16)
    gate_part = (grad_act * up_val * sigma_gate * (1.0 + gate_val * (1.0 - sigma_gate))).astype(
        jnp.bfloat16
    )
    back_width = model_width // BACK_PIECES
    normed_pieces = []
    for i in range(BACK_PIECES):
        rows = slice(i * back_width, (i + 1) * back_width)
        back_rows = lax.dot_general(
            gate_part, gate_mat[rows], LAST_DIMS, preferred_element_type=jnp.float32
        ) + lax.dot_general(up_part, up_mat[rows], LAST_DIMS, preferred_element_type=jnp.float32)
        returned = exchange(back_rows.astype(jnp.bfloat16))
        group_back = lax.dot_general(
            picker, returned, ROWS_DIMS, preferred_element_type=jnp.float32
        ).astype(jnp.bfloat16)
        normed_pieces.append(
            lax.psum_scatter(group_back, "exp", scatter_dimension=0, tiled=True)
        )
    all_inputs = jnp.concatenate(inputs, axis=1)
    all_upstream = jnp.concatenate(upstream, axis=1)
    down_grad = lax.dot_general(
        act_rows, all_upstream, ROWS_DIMS, preferred_element_type=jnp.float32
    ).astype(jnp.bfloat16)[None]
    gate_grad = lax.dot_general(
        all_inputs, gate_part, ROWS_DIMS, preferred_element_type=jnp.float32
    ).astype(jnp.bfloat16)[None]
    up_grad = lax.dot_general(
        all_inputs, up_part, ROWS_DIMS, preferred_element_type=jnp.float32
    ).astype(jnp.bfloat16)[None]
    normed_pieces, down_grad, gate_grad, up_grad = lax.optimization_barrier(
        (normed_pieces, down_grad, gate_grad, up_grad)
    )
    normed_grad = jnp.concatenate(normed_pieces, axis=1).astype(jnp.float32)
    gain_terms = jnp.sum(normed_grad * unit_rows, axis=0)
    for axis in ("ctx", "head", "exp"):
        gain_terms = sum(direct_gather(gain_terms, axis))
    gain_grad = gain_terms
    scaled = normed_grad * norm_gain
    mixed_term = jnp.mean(scaled * unit_rows, axis=1, keepdims=True)
    hidden_rows = (
        out_rows.astype(jnp.float32) + inv_rms * (scaled - unit_rows * mixed_term)
    ).astype(jnp.bfloat16)
    hidden_grad = hidden_rows.reshape(hidden_state.shape)
    ctx_count = lax.axis_size("ctx")
    ctx_index = lax.axis_index("ctx")
    query_block = query_heads[0, :, :, 0, :]
    seq_count, block_len = (query_block.shape[0], query_block.shape[1])
    head_size = key_heads.shape[-1]
    per_key = query_block.shape[2] // head_size
    query_rows = heads_to_rows(query_block, per_key, head_size)
    row_count = query_rows.shape[1]
    score_scaling = head_size ** (-0.5)
    query_pos = ctx_index * block_len + jnp.tile(jnp.arange(block_len, dtype=jnp.int32), per_key)
    query_last = ctx_index * block_len + block_len - 1
    seq_len = block_len * ctx_count

    def piece_scores(key_piece):
        key_pos = jnp.arange(key_piece.shape[1], dtype=jnp.int32)
        allowed = key_pos[None, None, :] <= query_pos[None, :, None]
        attention_scores = (
            jnp.einsum("sqd,skd->sqk", query_rows, key_piece, preferred_element_type=jnp.float32)
            * score_scaling
        )
        return (attention_scores, allowed)

    initial = (
        jnp.full((seq_count, row_count), FLOOR_SCORE, jnp.float32),
        jnp.zeros((seq_count, row_count), jnp.float32),
        jnp.zeros((seq_count, row_count, head_size), jnp.float32),
    )
    pieces = (
        lax.all_gather(key_heads, "ctx", axis=2, tiled=True),
        lax.all_gather(value_heads, "ctx", axis=2, tiled=True),
    )
    key_piece = pieces[0][0, :, :, 0, :]
    value_piece = pieces[1][0, :, :, 0, :]

    def forward_update(current):
        run_max, run_sum, run_acc = current
        attention_scores, allowed = piece_scores(key_piece)
        new_max = jnp.maximum(
            run_max, jnp.max(jnp.where(allowed, attention_scores, FLOOR_SCORE), axis=2)
        )
        weight_matrices = jnp.where(allowed, jnp.exp(attention_scores - new_max[:, :, None]), 0.0)
        new_sum = jnp.sum(weight_matrices, axis=2)
        new_acc = jnp.einsum(
            "sqk,skd->sqd",
            weight_matrices,
            value_piece.astype(jnp.float32),
            precision=lax.Precision.HIGHEST,
        )
        return (new_max, new_sum, new_acc)

    run_max, run_sum, run_acc = forward_update(initial)
    log_sum = run_max + jnp.log(run_sum)
    attn_rows = (run_acc / run_sum[:, :, None]).astype(jnp.bfloat16)
    grad_tokens = jnp.concatenate(direct_gather(hidden_rows, "head"), axis=0)
    proj_mat = out_weight[0]
    attn_grad_tok = lax.dot_general(
        grad_tokens, proj_mat, LAST_DIMS, preferred_element_type=jnp.float32
    ).astype(jnp.bfloat16)
    attention_gradient = heads_to_rows(
        attn_grad_tok.reshape(seq_count, block_len, per_key * head_size), per_key, head_size
    )
    delta_rows = jnp.sum(
        attention_gradient.astype(jnp.float32) * attn_rows.astype(jnp.float32), axis=2
    )
    attn_tokens = rows_to_heads(attn_rows, per_key, block_len).reshape(
        seq_count * block_len, per_key * head_size
    )
    initial_grads = (
        jnp.zeros((seq_count, row_count, head_size), jnp.float32),
        jnp.zeros((seq_count, seq_len, head_size), jnp.float32),
        jnp.zeros((seq_count, seq_len, head_size), jnp.float32),
    )

    def backward_update(current):
        attention_scores, allowed = piece_scores(key_piece)
        probability_values = jnp.where(
            allowed, jnp.exp(attention_scores - log_sum[:, :, None]), 0.0
        )
        value_part = jnp.einsum(
            "sqk,sqd->skd",
            probability_values.astype(jnp.bfloat16),
            attention_gradient,
            preferred_element_type=jnp.float32,
        )
        probability_gradient = jnp.einsum(
            "sqd,skd->sqk",
            attention_gradient,
            value_piece,
            preferred_element_type=jnp.float32,
        )
        score_gradient = (
            probability_values * (probability_gradient - delta_rows[:, :, None])
        ).astype(jnp.bfloat16)
        query_acc = (
            jnp.einsum(
                "sqk,skd->sqd",
                score_gradient,
                key_piece,
                preferred_element_type=jnp.float32,
            )
            * score_scaling
        )
        key_part = (
            jnp.einsum(
                "sqk,sqd->skd", score_gradient, query_rows, preferred_element_type=jnp.float32
            )
            * score_scaling
        )
        return (query_acc, key_part, value_part)

    query_acc, key_acc, value_acc = backward_update(initial_grads)
    proj_full = lax.dot_general(
        attn_tokens, grad_tokens, ROWS_DIMS, preferred_element_type=jnp.float32
    )
    def by_position(terms):
        return terms.reshape(seq_count, ctx_count, block_len, head_size).transpose(1, 0, 2, 3)

    exp_rows = proj_full.shape[0] // (ctx_count * exp_count)
    proj_mid = direct_scatter(
        proj_full.reshape(ctx_count, exp_count * exp_rows, model_width), "ctx"
    )
    proj_part = direct_scatter(proj_mid.reshape(exp_count, exp_rows, model_width), "exp").astype(
        jnp.bfloat16
    )
    key_total = direct_scatter(by_position(key_acc), "ctx")
    value_total = direct_scatter(by_position(value_acc), "ctx")
    query_gradient = (
        rows_to_heads(query_acc, per_key, block_len).astype(jnp.bfloat16).reshape(query_heads.shape)
    )
    key_gradient = key_total.astype(jnp.bfloat16).reshape(key_heads.shape)
    value_gradient = value_total.astype(jnp.bfloat16).reshape(value_heads.shape)
    proj_grad = proj_part[None]
    return (
        query_gradient,
        key_gradient,
        value_gradient,
        hidden_grad,
        gain_grad,
        proj_grad,
        gate_grad,
        up_grad,
        down_grad,
    )


def solution(mesh):
    return jax.shard_map(
        on_device,
        mesh=mesh,
        in_specs=(
            P("exp", None, "ctx", "head", None),
            P("exp", None, "ctx", "head", None),
            P("exp", None, "ctx", "head", None),
            P("exp", "head", "ctx", None),
            P("exp", "head", "ctx", None),
            P(),
            P("exp", "head", "ctx", None),
            P("exp", "head", "ctx", None),
            P("head", None, None),
            P(("ctx", "head", "exp"), None, None),
            P(("ctx", "head", "exp"), None, None),
            P(("ctx", "head", "exp"), None, None),
        ),
        out_specs=(
            P("exp", None, "ctx", "head", None),
            P("exp", None, "ctx", "head", None),
            P("exp", None, "ctx", "head", None),
            P("exp", "head", "ctx", None),
            P(),
            P("head", ("ctx", "exp"), None),
            P(("ctx", "head", "exp"), None, None),
            P(("ctx", "head", "exp"), None, None),
            P(("ctx", "head", "exp"), None, None),
        ),
        check_vma=False,
    )
```
